256 devices in a mesh: batch: 16 (over z, y_hi), feat: 16 (over x, y_lo, core).
Axes of the slice: x: 4, y: 4 (y_hi: 2, y_lo: 2; y = y_hi * 2 + y_lo), z: 8, core: 2. Of those that a mesh axis runs over, the one named last changes fastest.
Arguments:
- view_one: float32 [3072, 16384], P('batch', 'feat'), may hold values from -70 to 70
- view_two: float32 [3072, 16384], P('batch', 'feat'), may hold values from -70 to 70
Outputs:
- loss: float32 [], replicated
- grad_one: float32 [3072, 16384], P('batch', 'feat')
- grad_two: float32 [3072, 16384], P('batch', 'feat')
The draws below stay inside these ranges and needn't reach their ends.
All inputs are finite; a program needn't handle non-finite values.
Results may differ from the reference program's by a relative error of at most 0.0003.
Values sent between devices are 32-bit elements; how exact they have to be, the bound alone decides.
No kernel may reach another device: no remote copies, remote signals or barrier semaphores. Data moves between devices by JAX's collectives and lax.ppermute only.
A program may use at most 128 MiB of HBM per device.

```python
import jax
import jax.numpy as jnp
from jax import lax

FEATS = 16384
SAMPLES = 3072
FBLOCK = 1024
N_FEAT = 16


def common_parts(key, col_spread, row_spread):
    keys = jax.random.split(key, 5)
    normal_base = jnp.clip(jax.random.normal(keys[0], (SAMPLES, FEATS), jnp.float32), -4.0, 4.0)
    base = normal_base
    column_scale = jnp.exp(jax.random.uniform(keys[2], (1, FEATS), jnp.float32, minval=-col_spread, maxval=col_spread))
    offsets = jax.random.uniform(keys[3], (1, FEATS), jnp.float32, minval=-1.5, maxval=1.5)
    row_scale = jnp.exp(jax.random.uniform(keys[4], (SAMPLES, 1), jnp.float32, minval=-row_spread, maxval=row_spread))
    return (offsets, column_scale * row_scale, base)


def draw_view_one(key, part):
    offsets, scales, base = common_parts(key, 1.2, 0.4)
    return (offsets + scales * base).astype(jnp.float32)


def draw_view_two(key, part):
    offsets, scales, base = common_parts(key, 1.2, 0.4)
    own_key = jax.random.fold_in(key, 11)
    noise = 0.6 * jnp.clip(jax.random.normal(own_key, (SAMPLES, FEATS), jnp.float32), -4.0, 4.0)
    return (offsets + scales * (base + noise)).astype(jnp.float32)


def setup_inputs(seed: int = 0) -> dict:
    arg_keys = jax.random.split(jax.random.key(seed), 3)
    view_one = draw_view_one(jax.random.fold_in(arg_keys[2], 71), 0)
    view_two = draw_view_two(jax.random.fold_in(arg_keys[2], 71), 0)
    return dict(view_one=view_one, view_two=view_two)


def view_terms(view):
    count = view.shape[0]
    centred = view - lax.optimization_barrier(jnp.sum(view, axis=0)) / count
    deviation = jnp.sqrt(lax.optimization_barrier(jnp.sum(centred * centred, axis=0)) / (count - 1) + 0.0001)
    hinge_mean = jnp.mean(jnp.maximum(1.0 - deviation, 0.0))
    var_grad = -(25.0 * count / (8.0 * (count - 1))) * jnp.where(deviation < 1.0, centred / deviation, 0.0)

    def block_terms(block_index):
        block_cols = lax.dynamic_slice_in_dim(centred, (block_index * FBLOCK).astype(jnp.int32), FBLOCK, 1)
        cov_rows = jnp.dot(block_cols.T, centred, precision=lax.Precision.HIGHEST, preferred_element_type=jnp.float32) / (count - 1)
        row_ids = jnp.arange(FBLOCK, dtype=jnp.int32)[:, None] + block_index * FBLOCK
        col_ids = jnp.arange(FEATS, dtype=jnp.int32)[None, :]
        cov_rows = jnp.where(row_ids == col_ids, 0.0, cov_rows)
        square_sum = jnp.sum(cov_rows * cov_rows)
        grad_block = jnp.dot(centred, cov_rows.T, precision=lax.Precision.HIGHEST, preferred_element_type=jnp.float32) * (count / (count - 1.0))
        return (square_sum, grad_block)
    square_sums, grad_blocks = lax.map(block_terms, jnp.arange(N_FEAT, dtype=jnp.int32))
    cov_grad = jnp.transpose(grad_blocks, (1, 0, 2)).reshape(count, FEATS)
    cov_loss = jnp.sum(square_sums) / FEATS
    return (hinge_mean, var_grad, cov_loss, cov_grad)

def reference(view_one, view_two):
    hinge_one, var_one, cov_one, cgrad_one = view_terms(view_one)
    hinge_two, var_two, cov_two, cgrad_two = view_terms(view_two)
    differ = view_one - view_two
    loss = 25.0 * jnp.mean(differ * differ) + 12.5 * (hinge_one + hinge_two) + cov_one + cov_two
    grad_one = 12.5 * differ + var_one + cgrad_one
    grad_two = -12.5 * differ + var_two + cgrad_two
    return (loss, grad_one, grad_two)
```

```python
import jax
import jax.numpy as jnp
from jax import lax
from jax.sharding import PartitionSpec as P

Z = 8
X = 4


def z_send(value, steps):
    return lax.ppermute(value, "batch", [(b, (b + 2 * steps) % 16) for b in range(16)])


def y_swap(value):
    return lax.ppermute(value, "batch", [(b, b ^ 1) for b in range(16)])


def core_swap(value):
    return lax.ppermute(value, "feat", [(f, f ^ 1) for f in range(16)])


def lo_swap(value):
    return lax.ppermute(value, "feat", [(f, f ^ 2) for f in range(16)])


def x_send(value, steps):
    return lax.ppermute(value, "feat", [(f, (f + 4 * steps) % 16) for f in range(16)])


def z_sum(value):
    return sum([z_send(value, s) for s in range(1, Z)], value)


def x_sum(value):
    return sum([x_send(value, s) for s in range(1, X)], value)


def outer(left, right):
    return lax.dot_general(
        left, right, (((1,), (1,)), ((), ())), precision=lax.Precision.HIGH, preferred_element_type=jnp.float32
    )


def apply_rows(gram, rows):
    return lax.dot_general(
        gram, rows, (((1,), (0,)), ((), ())), precision=lax.Precision.HIGH, preferred_element_type=jnp.float32
    )


def apply_cols(gram, rows):
    return lax.dot_general(
        gram, rows, (((0,), (0,)), ((), ())), precision=lax.Precision.HIGH, preferred_element_type=jnp.float32
    )


def pick(value, index):
    return lax.dynamic_index_in_dim(value, index, 1, keepdims=False)


def feat_scatter(blocks, x, lo, core):
    count, height, width = blocks.shape
    halves = blocks.reshape(count, 2, height // 2, width)
    half = pick(halves, core) + core_swap(pick(halves, 1 - core))
    quarters = half.reshape(count, X, height // 8, width)
    part = pick(quarters, x)
    for s in range(1, X):
        part = part + x_send(pick(quarters, (x + s) % X), s)
    pieces = part.reshape(count, 2, height // 16, width)
    return pick(pieces, lo) + lo_swap(pick(pieces, 1 - lo))


def pair_up(own, other, second):
    first = jnp.where(second == 0, own, other)
    last = jnp.where(second == 0, other, own)
    return jnp.concatenate([first, last], axis=1)


def feat_gather(pieces, x, lo, core):
    count, height, width = pieces.shape
    part = pair_up(pieces, lo_swap(pieces), lo)
    quarters = jnp.zeros((count, X, 2 * height, width), pieces.dtype)
    for s in range(X):
        moved = part if s == 0 else x_send(part, s)
        quarters = lax.dynamic_update_slice_in_dim(quarters, moved[:, None], (x - s) % X, 1)
    half = quarters.reshape(count, 8 * height, width)
    return pair_up(half, core_swap(half), core)


def shards(view_one, view_two):
    rows, width = view_one.shape
    samples = rows * 16
    feats = width * 16
    scale_back = samples - 1.0
    batch = lax.axis_index("batch")
    feat = lax.axis_index("feat")
    hi = batch % 2
    x, lo, core = feat // 4, (feat // 2) % 2, feat % 2
    half_width = width // 2

    sums = jnp.stack([jnp.sum(view_one, axis=0), jnp.sum(view_two, axis=0)])
    sums = z_sum(sums)
    native = jnp.where(hi == 0, view_one, view_two)
    other = jnp.where(hi == 0, view_two, view_one)
    extra = y_swap(other)
    own_sum = jnp.where(hi == 0, sums[0], sums[1])
    other_sum = jnp.where(hi == 0, sums[1], sums[0])
    mean = ((own_sum + y_swap(other_sum)) / samples)[None, :]
    mean_halves = (mean[:, :half_width], mean[:, half_width:])

    raw = {0: (native, extra)}
    for d in (1, 2):
        raw[-d] = tuple(z_send(part, 1) for part in raw[1 - d])
        raw[d] = tuple(z_send(part, -1) for part in raw[d - 1])
    far = []
    for cols in (slice(0, half_width), slice(half_width, width)):
        down = z_send(jnp.concatenate([part[:, cols] for part in raw[-2]]), 1)
        up = z_send(jnp.concatenate([part[:, cols] for part in raw[2]]), -1)
        last = jnp.concatenate([z_send(down[:rows], 1), z_send(up[rows:], -1)])
        far.append({-3: down, 3: up, 4: last})

    near = {d: jnp.concatenate(raw[d]) - mean for d in range(-2, 3)}

    spread = z_sum(jnp.sum(near[0] * near[0], axis=0, keepdims=True))
    variance = spread / scale_back
    deviation = jnp.sqrt(variance + 0.0001)
    differ = view_one - view_two

    close = jnp.stack([outer(near[0], near[0]), outer(near[0], near[1]), outer(near[-1], near[1])])
    close = feat_scatter(close, x, lo, core)
    wide = jnp.stack([outer(near[-1], near[2]), outer(near[-2], near[2])])
    wide = feat_scatter(wide, x, lo, core)

    weight = jnp.array([1.0, 2.0, 2.0], jnp.float32)[:, None, None]
    wide_weight = jnp.array([2.0, 1.0], jnp.float32)[:, None, None]
    gram_square = jnp.sum(close * close * weight) + jnp.sum(wide * wide * wide_weight)
    loss = (
        25.0 * jnp.sum(differ * differ) / (samples * feats)
        + 12.5 * jnp.sum(jnp.maximum(1.0 - deviation, 0.0)) / (Z * feats)
        + gram_square / (scale_back * scale_back * feats)
        - jnp.sum(variance * variance) / (Z * feats)
    )
    row_ids = lax.broadcasted_iota(jnp.int32, (8, 128), 0)
    loss = jnp.full((8, 128), loss, jnp.float32)
    loss = loss + core_swap(loss)
    loss = loss + lo_swap(loss)
    loss = x_sum(jnp.where(row_ids == x, loss, 0.0))
    loss = jnp.broadcast_to(jnp.sum(loss, axis=0, keepdims=True), (8, 128))
    loss = z_sum(jnp.where(row_ids == batch // 2, loss, 0.0))
    loss = jnp.broadcast_to(jnp.sum(loss, axis=0, keepdims=True), (8, 128))
    loss = loss + y_swap(loss)

    from_below = z_send(close[1:3], 1)
    from_above = z_send(close[2:3], -1)
    close = feat_gather(jnp.concatenate([close[:2], from_above, from_below]), x, lo, core)
    three_up = z_send(wide[:1], -1)
    three_down = z_send(wide[:1], 2)
    four = z_send(wide[1:], -2)
    wide = feat_gather(jnp.concatenate([three_up, four, three_down]), x, lo, core)

    results = []
    for index, cols in enumerate((slice(0, half_width), slice(half_width, width))):
        far_rows = {d: value - mean_halves[index] for d, value in far[index].items()}
        product = apply_rows(close[0], near[0][:, cols])
        product = product + apply_rows(close[1], near[1][:, cols])
        product = product + apply_rows(close[2], near[2][:, cols])
        product = product + apply_cols(close[3], near[-1][:, cols])
        product = product + apply_cols(close[4], near[-2][:, cols])
        product = product + apply_rows(wide[0], far_rows[3])
        product = product + apply_rows(wide[1], far_rows[4])
        product = product + apply_cols(wide[2], far_rows[-3])
        centred = near[0][:, cols]
        var = variance[:, cols]
        dev = deviation[:, cols]
        grad = samples / (scale_back * scale_back) * (product - scale_back * centred * var)
        grad = grad - (25.0 * samples / (8.0 * (samples - 1))) * jnp.where(dev < 1.0, centred / dev, 0.0)
        back = y_swap(grad[rows:])
        apart = 12.5 * differ[:, cols]
        mine = grad[:rows]
        results.append(
            (apart + jnp.where(hi == 0, mine, back), jnp.where(hi == 0, back, mine) - apart)
        )
    grad_one = jnp.concatenate([r[0] for r in results], axis=1)
    grad_two = jnp.concatenate([r[1] for r in results], axis=1)
    return (loss[0, 0], grad_one, grad_two)


def solution(mesh):
    in_specs = (P("batch", "feat"), P("batch", "feat"))
    out_specs = (P(), P("batch", "feat"), P("batch", "feat"))
    return jax.shard_map(shards, mesh=mesh, in_specs=in_specs, out_specs=out_specs, check_vma=False)
```

```python
import functools

import jax
import jax.numpy as jnp
from jax import lax
from jax.experimental import pallas as pl
from jax.experimental.pallas import tpu as pltpu
from jax.sharding import PartitionSpec as P

Z = 8
X = 4


def z_send(value, steps):
    return lax.ppermute(value, "batch", [(b, (b + 2 * steps) % 16) for b in range(16)])


def y_swap(value):
    return lax.ppermute(value, "batch", [(b, b ^ 1) for b in range(16)])


def core_swap(value):
    return lax.ppermute(value, "feat", [(f, f ^ 1) for f in range(16)])


def lo_swap(value):
    return lax.ppermute(value, "feat", [(f, f ^ 2) for f in range(16)])


def x_send(value, steps):
    return lax.ppermute(value, "feat", [(f, (f + 4 * steps) % 16) for f in range(16)])


def z_swap(value, bit):
    return lax.ppermute(value, "batch", [(b, b ^ (2 * bit)) for b in range(16)])


def x_swap(value, bit):
    return lax.ppermute(value, "feat", [(f, f ^ (4 * bit)) for f in range(16)])


def after(value, *earlier):
    return lax.optimization_barrier((value, *earlier))[0]


def merge(stats, other, count):
    apart = other[0] - stats[0]
    return jnp.stack([0.5 * (stats[0] + other[0]), stats[1] + other[1] + (0.5 * count) * apart * apart])


FREE = pl.CostEstimate(flops=0, bytes_accessed=0, transcendentals=0)
ROOMY = pltpu.CompilerParams(vmem_limit_bytes=58 * 1024 * 1024)
PARAMS = pltpu.CompilerParams(vmem_limit_bytes=40 * 1024 * 1024)
WHOLE = pl.BlockSpec(memory_space=pltpu.VMEM)
SCALARS = pl.BlockSpec(memory_space=pltpu.SMEM)
ANY = pl.BlockSpec(memory_space=pl.ANY)


def split(value):
    high = value.astype(jnp.bfloat16)
    return high, (value - high.astype(jnp.float32)).astype(jnp.bfloat16)


def three_pass(left, right, dims):
    def dot(a, b):
        return lax.dot_general(a, b, (dims, ((), ())), preferred_element_type=jnp.float32)

    return dot(left[0], right[0]) + (dot(left[0], right[1]) + dot(left[1], right[0]))


def gram_kernel(pairs, place_ref, mean_ref, *refs):
    own_ref, other_ref, high, low, full = refs[-5:]
    parts = refs[:-5]
    rows = parts[0].shape[0]
    mean = mean_ref[...]
    for index, part in enumerate(parts):
        block, begin = index // 2, (index % 2) * rows
        high[block, begin : begin + rows], low[block, begin : begin + rows] = split(part[...] - mean)
    core = place_ref[0]
    piece = own_ref.shape[2]
    for k, (a, b) in enumerate(pairs):
        full[...] = three_pass((high[a], low[a]), (high[b], low[b]), ((1,), (1,)))
        for x in range(X):
            own_ref[k, x] = full[pl.ds(pl.multiple_of((2 * x + core) * piece, piece), piece)]
            other_ref[k, x] = full[pl.ds(pl.multiple_of((2 * x + 1 - core) * piece, piece), piece)]


def gram_blocks(place, mean, blocks, pairs):
    parts = [part for block in blocks for part in block]
    rows, width = parts[0].shape
    out = jax.ShapeDtypeStruct((len(pairs), X, rows // 4, 2 * rows), jnp.float32)
    return pl.pallas_call(
        functools.partial(gram_kernel, pairs),
        out_shape=(out, out),
        in_specs=[SCALARS] + [WHOLE] * (1 + len(parts)),
        out_specs=(WHOLE, WHOLE),
        scratch_shapes=[
            pltpu.VMEM((len(blocks), 2 * rows, width), jnp.bfloat16),
            pltpu.VMEM((len(blocks), 2 * rows, width), jnp.bfloat16),
            pltpu.VMEM((2 * rows, 2 * rows), jnp.float32),
        ],
        compiler_params=PARAMS,
        cost_estimate=FREE,
    )(place, mean, *parts)


def turn_kernel(place_ref, own_ref, other_ref, *out_refs):
    x = place_ref[1]
    for s in range(X):
        out_refs[s][...] = own_ref[:, (x + s) % X] + other_ref[:, (x + s) % X]


def x_pieces(place, own, other):
    count, _, height, width = own.shape
    out = jax.ShapeDtypeStruct((count, height, width), jnp.float32)
    return pl.pallas_call(
        turn_kernel,
        out_shape=(out,) * X,
        in_specs=[SCALARS, WHOLE, WHOLE],
        out_specs=(WHOLE,) * X,
        compiler_params=PARAMS,
        cost_estimate=FREE,
    )(place, own, other)


def prepare_kernel(place_ref, one_ref, two_ref, native_ref, other_ref, stats_ref):
    first = place_ref[2] == 0
    one, two = one_ref[...], two_ref[...]
    for index, (value, out_ref) in enumerate(
        ((jnp.where(first, one, two), native_ref), (jnp.where(first, two, one), other_ref))
    ):
        average = jnp.sum(value, axis=0, keepdims=True) / value.shape[0]
        apart = value - average
        out_ref[...] = value
        stats_ref[0, index : index + 1] = average
        stats_ref[1, index : index + 1] = jnp.sum(apart * apart, axis=0, keepdims=True)


def prepare(place, view_one, view_two):
    rows, width = view_one.shape
    whole = jax.ShapeDtypeStruct(view_one.shape, jnp.float32)
    block = pl.BlockSpec((rows, width // 2), lambda i: (0, i))
    return pl.pallas_call(
        prepare_kernel,
        grid=(2,),
        out_shape=(whole, whole, jax.ShapeDtypeStruct((2, 2, width), jnp.float32)),
        in_specs=[SCALARS, block, block],
        out_specs=(block, block, pl.BlockSpec((2, 2, width // 2), lambda i: (0, 0, i))),
        compiler_params=ROOMY,
        cost_estimate=FREE,
    )(place, view_one, view_two)


def product_kernel(half, samples, place_ref, mean_ref, variance_ref, own_ref, pair_ref, *refs):
    mine_ref, back_ref, gram, held, total, sems = refs[-6:]
    parts = refs[:-6]
    rows, cols = mine_ref.shape
    width = mean_ref.shape[1]
    blocks, pieces, piece, gram_width = gram.shape
    begin = half * cols

    core, x = place_ref[0], place_ref[1]

    def copies(block):
        moves = []
        for s in range(X):
            spot = 2 * ((x + X - s) % X)
            for ref, side in ((own_ref, core), (pair_ref, 1 - core)):
                moves.append((ref.at[s, pl.ds(block * piece, piece)], gram.at[block, spot + side]))
        for side in range(2):
            part = parts[2 * block + side]
            if part.shape[1] == width:
                part = part.at[:, pl.ds(begin, cols)]
            moves.append((part, held.at[block, pl.ds(side * rows, rows)]))
        return [pltpu.make_async_copy(src, dst, sems.at[block, i]) for i, (src, dst) in enumerate(moves)]

    for block in range(blocks):
        for copy in copies(block):
            copy.start()
    mean = mean_ref[:, begin : begin + cols]
    variance = variance_ref[:, begin : begin + cols]
    for block in range(blocks):
        for copy in copies(block):
            copy.wait()
        turned = block in (4, 5, 6)
        matrix = gram[block].reshape(pieces * piece, gram_width)
        term = three_pass(
            split(matrix.T if turned else matrix), split(held[block] - mean), ((1,), (0,))
        )
        if block == 0:
            total[...] = term
        else:
            total[...] += term
    centred = held[0] - mean
    back = samples - 1.0
    deviation = jnp.sqrt(variance + 0.0001)
    grad = samples / (back * back) * (total[...] - back * centred * variance)
    grad = grad - (25.0 * samples / (8.0 * back)) * jnp.where(deviation < 1.0, centred / deviation, 0.0)
    mine_ref[...] = grad[:rows]
    back_ref[...] = grad[rows:]


def product_half(half, samples, place, own, pair, mean, variance, parts):
    rows = parts[0].shape[0]
    cols = mean.shape[1] // 2
    blocks = len(parts) // 2
    out = jax.ShapeDtypeStruct((rows, cols), jnp.float32)
    return pl.pallas_call(
        functools.partial(product_kernel, half, samples),
        out_shape=(out, out),
        in_specs=[SCALARS, WHOLE, WHOLE] + [ANY] * (2 + len(parts)),
        out_specs=(WHOLE, WHOLE),
        scratch_shapes=[
            pltpu.VMEM((blocks, 2 * X, own.shape[1] // blocks, own.shape[2]), jnp.float32),
            pltpu.VMEM((blocks, 2 * rows, cols), jnp.float32),
            pltpu.VMEM((2 * rows, cols), jnp.float32),
            pltpu.SemaphoreType.DMA((blocks, 2 * X + 2)),
        ],
        compiler_params=ROOMY,
        cost_estimate=FREE,
    )(place, mean, variance, own, pair, *parts)


def x_scatter(pieces):
    return pieces[0] + sum([x_send(pieces[s], s) for s in range(2, X)], x_send(pieces[1], 1))


def lo_sum(part):
    return part + lo_swap(part)


def feat_gather(rows, *earlier):
    own = after(jnp.stack([rows] + [x_send(rows, s) for s in range(1, X)]), *earlier)
    return own, core_swap(own)


def shards(view_one, view_two):
    rows, width = view_one.shape
    samples = rows * 16
    feats = width * 16
    scale_back = samples - 1.0
    batch = lax.axis_index("batch")
    feat = lax.axis_index("feat")
    hi = batch % 2
    x, core = feat // 4, feat % 2
    half_width = width // 2

    place = jnp.stack([core, x, hi]).astype(jnp.int32)

    native, other, both = prepare(place, view_one, view_two)
    extra = y_swap(other)

    raw = {0: (native, extra)}
    for d in (1, 2, 3):
        raw[-d] = tuple(z_send(part, 1) for part in raw[1 - d])
        raw[d] = tuple(z_send(part, -1) for part in raw[d - 1])

    def first(d):
        return raw[-d][0], raw[d][0]

    def second(d):
        return raw[-d][1], raw[d][1]

    for step, bit in enumerate((1, 2, 4)):
        both = merge(both, z_swap(both, bit), rows << step)
        if step == 1:
            both = after(both, *first(1))
    both = after(both, *second(1))
    stats = merge(both[:, 0], y_swap(both[:, 1]), Z * rows)
    mean = stats[0][None, :]
    variance = stats[1][None, :] / scale_back
    deviation = jnp.sqrt(variance + 0.0001)
    differ = view_one - view_two

    own, other = gram_blocks(place, after(mean, *first(2)), [raw[0], raw[1], raw[-1]], ((0, 0), (0, 1), (2, 1)))
    close = x_scatter(x_pieces(place, *after((own, core_swap(other)), *second(2))))
    own, other = gram_blocks(place, mean, [raw[-2], raw[-1], raw[2]], ((1, 2), (0, 2)))
    wide = x_scatter(x_pieces(place, *after((own, core_swap(other)), *first(3))))
    gram = jnp.concatenate([lo_sum(close), lo_sum(after(wide, *second(3)))])
    count, height, width_rows = gram.shape
    gram = after(gram, raw[-3][1], raw[3][1])
    to_below = z_send(gram[2:4], -1)
    to_above = z_send(gram[1:3], 1)
    far_above = z_send(gram[3:4], 2)
    far_below = z_send(gram[4:], -2)
    sent = to_below, to_above, far_above, far_below
    last = z_send(after(raw[-3][0], *sent), 1), z_send(after(raw[3][1], *sent), -1)

    weight = jnp.array([1.0, 2.0, 2.0, 2.0, 1.0], jnp.float32)[:, None, None]
    loss = (
        25.0 * jnp.sum(differ * differ) / (samples * feats)
        + 12.5 * jnp.sum(jnp.maximum(1.0 - deviation, 0.0)) / (Z * feats)
        + jnp.sum(gram * gram * weight) / (2 * scale_back * scale_back * feats)
        - jnp.sum(variance * variance) / (Z * feats)
    )
    loss = jnp.full((8, 128), loss, jnp.float32)
    loss = loss + core_swap(loss)
    loss = loss + lo_swap(loss)
    for bit in (1, 2):
        loss = loss + x_swap(loss, bit)
    feat_loss = loss
    loss = after(loss + y_swap(loss), *last)
    for bit in (1, 2):
        loss = loss + z_swap(loss, bit)
    early = loss
    loss = loss + z_swap(loss, 4)
    later = loss

    gram = jnp.concatenate([gram[:2], to_below, to_above, far_above, far_below])
    own, pair = feat_gather(after(gram.reshape(8 * height, width_rows), feat_loss), *last, early)
    pair = after(pair, later)

    results = []
    for index, cols in enumerate((slice(0, half_width), slice(half_width, width))):
        parts = [part for d in (0, 1, 2, 3, -1, -2, -3) for part in raw[d]]
        mine, back = product_half(index, samples, place, own, pair, mean, variance, [*parts, *last])
        back = y_swap(back)
        apart = 12.5 * differ[:, cols]
        results.append(
            (apart + jnp.where(hi == 0, mine, back), jnp.where(hi == 0, back, mine) - apart)
        )
    grad_one = jnp.concatenate([r[0] for r in results], axis=1)
    grad_two = jnp.concatenate([r[1] for r in results], axis=1)
    return (loss[0, 0], grad_one, grad_two)


def solution(mesh):
    in_specs = (P("batch", "feat"), P("batch", "feat"))
    out_specs = (P(), P("batch", "feat"), P("batch", "feat"))
    return jax.shard_map(shards, mesh=mesh, in_specs=in_specs, out_specs=out_specs, check_vma=False)
```

```python
import functools

import jax
import jax.numpy as jnp
from jax import lax
from jax.experimental import pallas as pl
from jax.experimental.pallas import tpu as pltpu
from jax.sharding import PartitionSpec as P

Z = 8
X = 4


def z_send(value, steps):
    return lax.ppermute(value, "batch", [(b, (b + 2 * steps) % 16) for b in range(16)])


def y_swap(value):
    return lax.ppermute(value, "batch", [(b, b ^ 1) for b in range(16)])


def core_swap(value):
    return lax.ppermute(value, "feat", [(f, f ^ 1) for f in range(16)])


def lo_swap(value):
    return lax.ppermute(value, "feat", [(f, f ^ 2) for f in range(16)])


def x_send(value, steps):
    return lax.ppermute(value, "feat", [(f, (f + 4 * steps) % 16) for f in range(16)])


def z_swap(value, bit):
    return lax.ppermute(value, "batch", [(b, b ^ (2 * bit)) for b in range(16)])


def x_swap(value, bit):
    return lax.ppermute(value, "feat", [(f, f ^ (4 * bit)) for f in range(16)])


def after(value, *earlier):
    return lax.optimization_barrier((value, *earlier))[0]


def merge(stats, other, count):
    apart = other[0] - stats[0]
    return jnp.stack([0.5 * (stats[0] + other[0]), stats[1] + other[1] + (0.5 * count) * apart * apart])


FREE = pl.CostEstimate(flops=0, bytes_accessed=0, transcendentals=0)
ROOMY = pltpu.CompilerParams(vmem_limit_bytes=58 * 1024 * 1024)
PARAMS = pltpu.CompilerParams(vmem_limit_bytes=40 * 1024 * 1024)
WHOLE = pl.BlockSpec(memory_space=pltpu.VMEM)
SCALARS = pl.BlockSpec(memory_space=pltpu.SMEM)
ANY = pl.BlockSpec(memory_space=pl.ANY)


def split(value):
    high = value.astype(jnp.bfloat16)
    return high, (value - high.astype(jnp.float32)).astype(jnp.bfloat16)


def three_pass(left, right, dims):
    def dot(a, b):
        return lax.dot_general(a, b, (dims, ((), ())), preferred_element_type=jnp.float32)

    return dot(left[0], right[0]) + (dot(left[0], right[1]) + dot(left[1], right[0]))


def gram_kernel(pairs, place_ref, mean_ref, *refs):
    own_ref, other_ref, high, low, full = refs[-5:]
    parts = refs[:-5]
    rows = parts[0].shape[0]
    mean = mean_ref[...]
    for index, part in enumerate(parts):
        block, begin = index // 2, (index % 2) * rows
        high[block, begin : begin + rows], low[block, begin : begin + rows] = split(part[...] - mean)
    core = place_ref[0]
    piece = own_ref.shape[2]
    for k, (a, b) in enumerate(pairs):
        full[...] = three_pass((high[a], low[a]), (high[b], low[b]), ((1,), (1,)))
        for x in range(X):
            own_ref[k, x] = full[pl.ds(pl.multiple_of((2 * x + core) * piece, piece), piece)]
            other_ref[k, x] = full[pl.ds(pl.multiple_of((2 * x + 1 - core) * piece, piece), piece)]


def gram_blocks(place, mean, blocks, pairs):
    parts = [part for block in blocks for part in block]
    rows, width = parts[0].shape
    out = jax.ShapeDtypeStruct((len(pairs), X, rows // 4, 2 * rows), jnp.float32)
    return pl.pallas_call(
        functools.partial(gram_kernel, pairs),
        out_shape=(out, out),
        in_specs=[SCALARS] + [WHOLE] * (1 + len(parts)),
        out_specs=(WHOLE, WHOLE),
        scratch_shapes=[
            pltpu.VMEM((len(blocks), 2 * rows, width), jnp.bfloat16),
            pltpu.VMEM((len(blocks), 2 * rows, width), jnp.bfloat16),
            pltpu.VMEM((2 * rows, 2 * rows), jnp.float32),
        ],
        compiler_params=PARAMS,
        cost_estimate=FREE,
    )(place, mean, *parts)


def turn_kernel(place_ref, own_ref, other_ref, *out_refs):
    x = place_ref[1]
    for s in range(X):
        out_refs[s][...] = own_ref[:, (x + s) % X] + other_ref[:, (x + s) % X]


def x_pieces(place, own, other):
    count, _, height, width = own.shape
    out = jax.ShapeDtypeStruct((count, height, width), jnp.float32)
    return pl.pallas_call(
        turn_kernel,
        out_shape=(out,) * X,
        in_specs=[SCALARS, WHOLE, WHOLE],
        out_specs=(WHOLE,) * X,
        compiler_params=PARAMS,
        cost_estimate=FREE,
    )(place, own, other)


def prepare_kernel(place_ref, one_ref, two_ref, native_ref, other_ref, stats_ref):
    first = place_ref[2] == 0
    one, two = one_ref[...], two_ref[...]
    for index, (value, out_ref) in enumerate(
        ((jnp.where(first, one, two), native_ref), (jnp.where(first, two, one), other_ref))
    ):
        average = jnp.sum(value, axis=0, keepdims=True) / value.shape[0]
        apart = value - average
        out_ref[...] = value
        stats_ref[0, index : index + 1] = average
        stats_ref[1, index : index + 1] = jnp.sum(apart * apart, axis=0, keepdims=True)


def prepare(place, view_one, view_two):
    rows, width = view_one.shape
    whole = jax.ShapeDtypeStruct(view_one.shape, jnp.float32)
    block = pl.BlockSpec((rows, width // 2), lambda i: (0, i))
    return pl.pallas_call(
        prepare_kernel,
        grid=(2,),
        out_shape=(whole, whole, jax.ShapeDtypeStruct((2, 2, width), jnp.float32)),
        in_specs=[SCALARS, block, block],
        out_specs=(block, block, pl.BlockSpec((2, 2, width // 2), lambda i: (0, 0, i))),
        compiler_params=ROOMY,
        cost_estimate=FREE,
    )(place, view_one, view_two)


def product_kernel(half, samples, place_ref, mean_ref, variance_ref, own_ref, pair_ref, *refs):
    mine_ref, back_ref, gram, held, total, sems = refs[-6:]
    parts = refs[:-6]
    rows, cols = mine_ref.shape
    width = mean_ref.shape[1]
    blocks, pieces, piece, gram_width = gram.shape
    begin = half * cols

    core, x = place_ref[0], place_ref[1]

    def copies(block):
        moves = []
        for s in range(X):
            spot = 2 * ((x + X - s) % X)
            for ref, side in ((own_ref, core), (pair_ref, 1 - core)):
                moves.append((ref.at[s, pl.ds(block * piece, piece)], gram.at[block, spot + side]))
        for side in range(2):
            part = parts[2 * block + side]
            if part.shape[1] == width:
                part = part.at[:, pl.ds(begin, cols)]
            moves.append((part, held.at[block, pl.ds(side * rows, rows)]))
        return [pltpu.make_async_copy(src, dst, sems.at[block, i]) for i, (src, dst) in enumerate(moves)]

    for block in range(blocks):
        for copy in copies(block):
            copy.start()
    mean = mean_ref[:, begin : begin + cols]
    variance = variance_ref[:, begin : begin + cols]
    for block in range(blocks):
        for copy in copies(block):
            copy.wait()
        turned = block in (4, 5, 6)
        matrix = gram[block].reshape(pieces * piece, gram_width)
        term = three_pass(
            split(matrix.T if turned else matrix), split(held[block] - mean), ((1,), (0,))
        )
        if block == 0:
            total[...] = term
        else:
            total[...] += term
    centred = held[0] - mean
    back = samples - 1.0
    deviation = jnp.sqrt(variance + 0.0001)
    grad = samples / (back * back) * (total[...] - back * centred * variance)
    grad = grad - (25.0 * samples / (8.0 * back)) * jnp.where(deviation < 1.0, centred / deviation, 0.0)
    mine_ref[...] = grad[:rows]
    back_ref[...] = grad[rows:]


def product_half(half, samples, place, own, pair, mean, variance, parts):
    rows = parts[0].shape[0]
    cols = mean.shape[1] // 2
    blocks = len(parts) // 2
    out = jax.ShapeDtypeStruct((rows, cols), jnp.float32)
    return pl.pallas_call(
        functools.partial(product_kernel, half, samples),
        out_shape=(out, out),
        in_specs=[SCALARS, WHOLE, WHOLE] + [ANY] * (2 + len(parts)),
        out_specs=(WHOLE, WHOLE),
        scratch_shapes=[
            pltpu.VMEM((blocks, 2 * X, own.shape[2] // (2 * X), own.shape[2]), jnp.float32),
            pltpu.VMEM((blocks, 2 * rows, cols), jnp.float32),
            pltpu.VMEM((2 * rows, cols), jnp.float32),
            pltpu.SemaphoreType.DMA((blocks, 2 * X + 2)),
        ],
        compiler_params=ROOMY,
        cost_estimate=FREE,
    )(place, mean, variance, own, pair, *parts)


def x_scatter(pieces):
    return pieces[0] + sum([x_send(pieces[s], s) for s in range(2, X)], x_send(pieces[1], 1))


def lo_sum(part):
    return part + lo_swap(part)


def feat_gather(rows, *earlier):
    own = after(jnp.stack([rows] + [x_send(rows, s) for s in range(1, X)]), *earlier)
    return own, core_swap(own)


def shards(view_one, view_two):
    rows, width = view_one.shape
    samples = rows * 16
    feats = width * 16
    scale_back = samples - 1.0
    batch = lax.axis_index("batch")
    feat = lax.axis_index("feat")
    hi = batch % 2
    x, core = feat // 4, feat % 2
    half_width = width // 2

    place = jnp.stack([core, x, hi]).astype(jnp.int32)

    native, other, both = prepare(place, view_one, view_two)
    extra = y_swap(other)

    raw = {0: (native, extra)}
    for d in (1, 2, 3):
        raw[-d] = tuple(z_send(part, 1) for part in raw[1 - d])
        raw[d] = tuple(z_send(part, -1) for part in raw[d - 1])

    def first(d):
        return raw[-d][0], raw[d][0]

    def second(d):
        return raw[-d][1], raw[d][1]

    for step, bit in enumerate((1, 2, 4)):
        both = merge(both, z_swap(both, bit), rows << step)
        if step == 1:
            both = after(both, *first(1))
    both = after(both, *second(1))
    stats = merge(both[:, 0], y_swap(both[:, 1]), Z * rows)
    mean = stats[0][None, :]
    variance = stats[1][None, :] / scale_back
    deviation = jnp.sqrt(variance + 0.0001)
    differ = view_one - view_two

    own, other = gram_blocks(place, after(mean, *first(2)), [raw[0], raw[1], raw[-1]], ((0, 0), (0, 1), (2, 1)))
    close = x_scatter(x_pieces(place, *after((own, core_swap(other)), *second(2))))
    own, other = gram_blocks(place, mean, [raw[-2], raw[-1], raw[2]], ((1, 2), (0, 2)))
    wide = x_scatter(x_pieces(place, *after((own, core_swap(other)), *first(3))))
    gram = jnp.concatenate([lo_sum(close), lo_sum(after(wide, *second(3)))])
    count, height, width_rows = gram.shape
    gram = after(gram, raw[-3][1], raw[3][1])
    to_below = z_send(gram[2:4], -1)
    to_above = z_send(gram[1:3], 1)
    far_above = z_send(gram[3:4], 2)
    far_below = z_send(gram[4:], -2)
    sent = to_below, to_above, far_above, far_below
    last = z_send(after(raw[-3][0], *sent), 1), z_send(after(raw[3][1], *sent), -1)

    weight = jnp.array([1.0, 2.0, 2.0, 2.0, 1.0], jnp.float32)[:, None, None]
    loss = (
        25.0 * jnp.sum(differ * differ) / (samples * feats)
        + 12.5 * jnp.sum(jnp.maximum(1.0 - deviation, 0.0)) / (Z * feats)
        - jnp.sum(variance * variance) / (Z * feats)
    )
    loss = lo_sum(jnp.full((8, 128), loss, jnp.float32))[0, 0]
    loss = loss + jnp.sum(gram * gram * weight) / (scale_back * scale_back * feats)

    gram = jnp.concatenate([gram[:2], to_below, to_above, far_above, far_below])
    lane = lax.broadcasted_iota(jnp.int32, (8, width_rows), 1)
    gram = jnp.concatenate([gram.reshape(8 * height, width_rows), jnp.where(lane == 2 * x + core, loss, 0.0)])
    own, pair = feat_gather(gram, *last)
    lanes = own[:, 8 * height, : 2 * X] + pair[:, 8 * height, : 2 * X]
    loss = jnp.full((8, 128), jnp.sum(jnp.sum(lanes, axis=0)), jnp.float32)
    loss = loss + y_swap(loss)
    for bit in (1, 2, 4):
        loss = loss + z_swap(loss, bit)

    results = []
    for index, cols in enumerate((slice(0, half_width), slice(half_width, width))):
        parts = [part for d in (0, 1, 2, 3, -1, -2, -3) for part in raw[d]]
        mine, back = product_half(index, samples, place, own, pair, mean, variance, [*parts, *last])
        back = y_swap(back)
        apart = 12.5 * differ[:, cols]
        results.append(
            (apart + jnp.where(hi == 0, mine, back), jnp.where(hi == 0, back, mine) - apart)
        )
    grad_one = jnp.concatenate([r[0] for r in results], axis=1)
    grad_two = jnp.concatenate([r[1] for r in results], axis=1)
    return (loss[0, 0], grad_one, grad_two)


def solution(mesh):
    in_specs = (P("batch", "feat"), P("batch", "feat"))
    out_specs = (P(), P("batch", "feat"), P("batch", "feat"))
    return jax.shard_map(shards, mesh=mesh, in_specs=in_specs, out_specs=out_specs, check_vma=False)
```

```python
import functools

import jax
import jax.numpy as jnp
from jax import lax
from jax.experimental import pallas as pl
from jax.experimental.pallas import tpu as pltpu
from jax.sharding import PartitionSpec as P

Z = 8
X = 4


def z_send(value, steps):
    return lax.ppermute(value, "batch", [(b, (b + 2 * steps) % 16) for b in range(16)])


def y_swap(value):
    return lax.ppermute(value, "batch", [(b, b ^ 1) for b in range(16)])


def core_swap(value):
    return lax.ppermute(value, "feat", [(f, f ^ 1) for f in range(16)])


def lo_swap(value):
    return lax.ppermute(value, "feat", [(f, f ^ 2) for f in range(16)])


def x_send(value, steps):
    return lax.ppermute(value, "feat", [(f, (f + 4 * steps) % 16) for f in range(16)])


def z_swap(value, bit):
    return lax.ppermute(value, "batch", [(b, b ^ (2 * bit)) for b in range(16)])


def x_swap(value, bit):
    return lax.ppermute(value, "feat", [(f, f ^ (4 * bit)) for f in range(16)])


def after(value, *earlier):
    return lax.optimization_barrier((value, *earlier))[0]


def merge(stats, other, count):
    apart = other[0] - stats[0]
    return jnp.stack([0.5 * (stats[0] + other[0]), stats[1] + other[1] + (0.5 * count) * apart * apart])


FREE = pl.CostEstimate(flops=0, bytes_accessed=0, transcendentals=0)
ROOMY = pltpu.CompilerParams(vmem_limit_bytes=58 * 1024 * 1024)
PARAMS = pltpu.CompilerParams(vmem_limit_bytes=40 * 1024 * 1024)
WHOLE = pl.BlockSpec(memory_space=pltpu.VMEM)
SCALARS = pl.BlockSpec(memory_space=pltpu.SMEM)
ANY = pl.BlockSpec(memory_space=pl.ANY)


def split(value):
    high = value.astype(jnp.bfloat16)
    return high, (value - high.astype(jnp.float32)).astype(jnp.bfloat16)


def three_pass(left, right, dims):
    def dot(a, b):
        return lax.dot_general(a, b, (dims, ((), ())), preferred_element_type=jnp.float32)

    return dot(left[0], right[0]) + (dot(left[0], right[1]) + dot(left[1], right[0]))


def gram_kernel(pairs, place_ref, mean_ref, *refs):
    own_ref, other_ref, high, low, full = refs[-5:]
    parts = refs[:-5]
    rows = parts[0].shape[0]
    mean = mean_ref[...]
    for index, part in enumerate(parts):
        block, begin = index // 2, (index % 2) * rows
        high[block, begin : begin + rows], low[block, begin : begin + rows] = split(part[...] - mean)
    core = place_ref[0]
    piece = own_ref.shape[2]
    for k, (a, b) in enumerate(pairs):
        full[...] = three_pass((high[a], low[a]), (high[b], low[b]), ((1,), (1,)))
        for x in range(X):
            own_ref[k, x] = full[pl.ds(pl.multiple_of((2 * x + core) * piece, piece), piece)]
            other_ref[k, x] = full[pl.ds(pl.multiple_of((2 * x + 1 - core) * piece, piece), piece)]


def gram_blocks(place, mean, blocks, pairs):
    parts = [part for block in blocks for part in block]
    rows, width = parts[0].shape
    out = jax.ShapeDtypeStruct((len(pairs), X, rows // 4, 2 * rows), jnp.float32)
    return pl.pallas_call(
        functools.partial(gram_kernel, pairs),
        out_shape=(out, out),
        in_specs=[SCALARS] + [WHOLE] * (1 + len(parts)),
        out_specs=(WHOLE, WHOLE),
        scratch_shapes=[
            pltpu.VMEM((len(blocks), 2 * rows, width), jnp.bfloat16),
            pltpu.VMEM((len(blocks), 2 * rows, width), jnp.bfloat16),
            pltpu.VMEM((2 * rows, 2 * rows), jnp.float32),
        ],
        compiler_params=PARAMS,
        cost_estimate=FREE,
    )(place, mean, *parts)


def turn_kernel(place_ref, own_ref, other_ref, *out_refs):
    x = place_ref[1]
    for s in range(X):
        out_refs[s][...] = own_ref[:, (x + s) % X] + other_ref[:, (x + s) % X]


def x_pieces(place, own, other):
    count, _, height, width = own.shape
    out = jax.ShapeDtypeStruct((count, height, width), jnp.float32)
    return pl.pallas_call(
        turn_kernel,
        out_shape=(out,) * X,
        in_specs=[SCALARS, WHOLE, WHOLE],
        out_specs=(WHOLE,) * X,
        compiler_params=PARAMS,
        cost_estimate=FREE,
    )(place, own, other)


def prepare_kernel(place_ref, one_ref, two_ref, native_ref, other_ref, stats_ref):
    first = place_ref[2] == 0
    one, two = one_ref[...], two_ref[...]
    for index, (value, out_ref) in enumerate(
        ((jnp.where(first, one, two), native_ref), (jnp.where(first, two, one), other_ref))
    ):
        average = jnp.sum(value, axis=0, keepdims=True) / value.shape[0]
        apart = value - average
        out_ref[...] = value
        stats_ref[0, index : index + 1] = average
        stats_ref[1, index : index + 1] = jnp.sum(apart * apart, axis=0, keepdims=True)


def prepare(place, view_one, view_two):
    rows, width = view_one.shape
    whole = jax.ShapeDtypeStruct(view_one.shape, jnp.float32)
    block = pl.BlockSpec((rows, width // 2), lambda i: (0, i))
    return pl.pallas_call(
        prepare_kernel,
        grid=(2,),
        out_shape=(whole, whole, jax.ShapeDtypeStruct((2, 2, width), jnp.float32)),
        in_specs=[SCALARS, block, block],
        out_specs=(block, block, pl.BlockSpec((2, 2, width // 2), lambda i: (0, 0, i))),
        compiler_params=ROOMY,
        cost_estimate=FREE,
    )(place, view_one, view_two)


def product_kernel(half, samples, place_ref, mean_ref, variance_ref, own_ref, pair_ref, *refs):
    mine_ref, back_ref, gram, held, total, sems = refs[-6:]
    parts = refs[:-6]
    rows, cols = mine_ref.shape
    width = mean_ref.shape[1]
    blocks, pieces, piece, gram_width = gram.shape
    begin = half * cols

    core, x = place_ref[0], place_ref[1]

    def copies(block):
        moves = []
        for s in range(X):
            spot = 2 * ((x + X - s) % X)
            for ref, side in ((own_ref, core), (pair_ref, 1 - core)):
                moves.append((ref.at[s, pl.ds(block * piece, piece)], gram.at[block, spot + side]))
        for side in range(2):
            part = parts[2 * block + side]
            if part.shape[1] == width:
                part = part.at[:, pl.ds(begin, cols)]
            moves.append((part, held.at[block, pl.ds(side * rows, rows)]))
        return [pltpu.make_async_copy(src, dst, sems.at[block, i]) for i, (src, dst) in enumerate(moves)]

    for block in range(blocks):
        for copy in copies(block):
            copy.start()
    mean = mean_ref[:, begin : begin + cols]
    variance = variance_ref[:, begin : begin + cols]
    for block in range(blocks):
        for copy in copies(block):
            copy.wait()
        turned = block in (4, 5, 6)
        matrix = gram[block].reshape(pieces * piece, gram_width)
        term = three_pass(
            split(matrix.T if turned else matrix), split(held[block] - mean), ((1,), (0,))
        )
        if block == 0:
            total[...] = term
        else:
            total[...] += term
    centred = held[0] - mean
    back = samples - 1.0
    deviation = jnp.sqrt(variance + 0.0001)
    grad = samples / (back * back) * (total[...] - back * centred * variance)
    grad = grad - (25.0 * samples / (8.0 * back)) * jnp.where(deviation < 1.0, centred / deviation, 0.0)
    mine_ref[...] = grad[:rows]
    back_ref[...] = grad[rows:]


def product_half(half, samples, place, own, pair, mean, variance, parts):
    rows = parts[0].shape[0]
    cols = mean.shape[1] // 2
    blocks = len(parts) // 2
    out = jax.ShapeDtypeStruct((rows, cols), jnp.float32)
    return pl.pallas_call(
        functools.partial(product_kernel, half, samples),
        out_shape=(out, out),
        in_specs=[SCALARS, WHOLE, WHOLE] + [ANY] * (2 + len(parts)),
        out_specs=(WHOLE, WHOLE),
        scratch_shapes=[
            pltpu.VMEM((blocks, 2 * X, own.shape[2] // (2 * X), own.shape[2]), jnp.float32),
            pltpu.VMEM((blocks, 2 * rows, cols), jnp.float32),
            pltpu.VMEM((2 * rows, cols), jnp.float32),
            pltpu.SemaphoreType.DMA((blocks, 2 * X + 2)),
        ],
        compiler_params=ROOMY,
        cost_estimate=FREE,
    )(place, mean, variance, own, pair, *parts)


def x_scatter(pieces):
    return pieces[0] + sum([x_send(pieces[s], s) for s in range(2, X)], x_send(pieces[1], 1))


def lo_sum(part):
    return part + lo_swap(part)


def feat_gather(rows, *earlier):
    own = after(jnp.stack([rows] + [x_send(rows, s) for s in range(1, X)]), *earlier)
    return own, core_swap(own)


def shards(view_one, view_two):
    rows, width = view_one.shape
    samples = rows * 16
    feats = width * 16
    scale_back = samples - 1.0
    batch = lax.axis_index("batch")
    feat = lax.axis_index("feat")
    hi = batch % 2
    x, core = feat // 4, feat % 2
    half_width = width // 2

    place = jnp.stack([core, x, hi]).astype(jnp.int32)

    native, other, both = prepare(place, view_one, view_two)
    extra = y_swap(other)

    raw = {0: (native, extra)}
    for d in (1, 2, 3):
        raw[-d] = tuple(z_send(part, 1) for part in raw[1 - d])
        raw[d] = tuple(z_send(part, -1) for part in raw[d - 1])

    def first(d):
        return raw[-d][0], raw[d][0]

    def second(d):
        return raw[-d][1], raw[d][1]

    for step, bit in enumerate((1, 2, 4)):
        both = merge(both, z_swap(both, bit), rows << step)
        if step == 1:
            both = after(both, *first(1))
    both = after(both, *second(1))
    stats = merge(both[:, 0], y_swap(both[:, 1]), Z * rows)
    mean = stats[0][None, :]
    variance = stats[1][None, :] / scale_back
    deviation = jnp.sqrt(variance + 0.0001)
    differ = view_one - view_two

    own, other = gram_blocks(place, after(mean, *first(2)), [raw[0], raw[1], raw[-1]], ((0, 0), (0, 1), (2, 1)))
    close = x_scatter(x_pieces(place, *after((own, core_swap(other)), *second(2))))
    own, other = gram_blocks(place, mean, [raw[-2], raw[-1], raw[2]], ((1, 2), (0, 2)))
    wide = x_scatter(x_pieces(place, *after((own, core_swap(other)), *first(3))))
    gram = jnp.concatenate([lo_sum(close), lo_sum(after(wide, *second(3)))])
    count, height, width_rows = gram.shape
    gram = after(gram, raw[-3][1], raw[3][1])
    to_below = z_send(gram[2:4], -1)
    to_above = z_send(gram[1:3], 1)
    far_above = z_send(gram[3:4], 2)
    far_below = z_send(gram[4:], -2)
    sent = to_below, to_above, far_above, far_below
    last = z_send(after(raw[-3][0], *sent), 1), z_send(after(raw[3][1], *sent), -1)

    weight = jnp.array([1.0, 2.0, 2.0, 2.0, 1.0], jnp.float32)[:, None, None]
    loss = (
        25.0 * jnp.sum(differ * differ) / (samples * feats)
        + 12.5 * jnp.sum(jnp.maximum(1.0 - deviation, 0.0)) / (Z * feats)
        - jnp.sum(variance * variance) / (Z * feats)
    )
    loss = lo_sum(jnp.full((8, 128), loss, jnp.float32))[0, 0]
    loss = loss + jnp.sum(gram * gram * weight) / (scale_back * scale_back * feats)

    gram = jnp.concatenate([gram[:2], to_below, to_above, far_above, far_below])
    lane = lax.broadcasted_iota(jnp.int32, (8, width_rows), 1)
    gram = jnp.concatenate([gram.reshape(8 * height, width_rows), jnp.where(lane == 2 * x + core, loss, 0.0)])
    own, pair = feat_gather(gram, *last)
    lanes = own[:, 8 * height, : 2 * X] + pair[:, 8 * height, : 2 * X]
    loss = jnp.full((8, 128), jnp.sum(jnp.sum(lanes, axis=0)), jnp.float32)
    loss = loss + y_swap(loss)
    means = [mean]
    for bit in (1, 2, 4):
        loss = loss + z_swap(loss, bit)
        means.append(after(mean, loss))

    results = []
    for index, cols in enumerate((slice(0, half_width), slice(half_width, width))):
        parts = [part for d in (0, 1, 2, 3, -1, -2, -3) for part in raw[d]]
        mine, back = product_half(index, samples, place, own, pair, means[index], variance, [*parts, *last])
        back = y_swap(back)
        apart = 12.5 * differ[:, cols]
        results.append(
            (apart + jnp.where(hi == 0, mine, back), jnp.where(hi == 0, back, mine) - apart)
        )
    grad_one = jnp.concatenate([r[0] for r in results], axis=1)
    grad_two = jnp.concatenate([r[1] for r in results], axis=1)
    return (loss[0, 0], grad_one, grad_two)


def solution(mesh):
    in_specs = (P("batch", "feat"), P("batch", "feat"))
    out_specs = (P(), P("batch", "feat"), P("batch", "feat"))
    return jax.shard_map(shards, mesh=mesh, in_specs=in_specs, out_specs=out_specs, check_vma=False)
```
